32 devices in a mesh: member: 4 (over x, core), space: 8 (over z, y).
Axes of the slice: x: 2, y: 2, z: 4, core: 2. Of those that a mesh axis runs over, the one named last changes fastest.
Arguments:
- members: bfloat16 [64, 32, 128, 384], P('member', None, 'space'), may hold values from -6 to 6
- control: float32 [32, 128, 384], P(None, 'space'), may hold values from -6 to 6
- hybrid_weight: float32 [32], replicated, may hold values from 0.2 to 0.6
- member_weights: int32 [64], replicated, may hold values from 1 to 8
- source_device: int32 [128, 1], P('space'), may hold values from 0 to 7, as said below
- source_row: int32 [128], P('space'), may hold values from 0 to 15
- column_source: int32 [128, 768], P('space'), may hold values from 0 to 382, as said below
- column_code: int32 [128, 768], P('space'), may hold values from 0 to 16
Outputs:
- fine_increment: float32 [128, 32, 2, 768], P('space', 'member')
The draws below stay inside these ranges and needn't reach their ends.
Inputs may be any that keep to these rules, and one draw needn't show every extreme that they name: `source_device`: among the 16 fine blocks of one device no space index is named more than 4 times, and in every draw some device's blocks name some index exactly 4 times. `column_source`: within 2 of (j - 1) // 2 for fine column j, clipped to the range.
All inputs are finite; a program needn't handle non-finite values.
Results may differ from the reference program's by a relative error of at most 0.0022.
Values sent between devices are 32-bit elements; how exact they have to be, the bound alone decides.
A program may use at most 128 MiB of HBM per device.

```python
import math
import jax
import jax.numpy as jnp
from jax import lax

NX = 384
FX = 768
SWEEPS = 4
ROWS_DEV = 16
C = 32
MEMBERS = 64
NY = 128
CAP = 4
N_SPACE = 8


def block_owners(key):
    order = jax.random.permutation(jax.random.fold_in(key, 7), N_SPACE).astype(jnp.int32)
    blocks = jnp.arange(NY, dtype=jnp.int32)
    return jnp.take(order, blocks // CAP % N_SPACE).astype(jnp.int32)


def draw_source_device(key, part):
    return block_owners(key)[:, None].astype(jnp.int32)


def draw_source_row(key, part):
    blocks = jnp.arange(NY, dtype=jnp.int32)
    random_rows = jax.random.randint(jax.random.fold_in(key, 11), (NY,), 0, ROWS_DEV, dtype=jnp.int32)
    leading = blocks % CAP == 0
    return jnp.where(leading, ROWS_DEV - 1, random_rows).astype(jnp.int32)


def draw_column_source(key, part):
    columns = jnp.arange(FX, dtype=jnp.int32)
    centre = (columns - 1) // 2
    jitter = jax.random.randint(key, (NY, FX), -2, 3, dtype=jnp.int32)
    return jnp.clip(centre[None, :] + jitter, 0, NX - 2).astype(jnp.int32)


def draw_members(key, part):
    rows = jnp.arange(NY, dtype=jnp.float32)[:, None]
    phase = rows * (2.0 * math.pi / 64.0)
    small_shape = (MEMBERS, C, 1, NX)
    full_shape = (MEMBERS, C, NY, NX)
    first = jax.random.normal(jax.random.fold_in(key, 21), small_shape, jnp.float32)
    second = jax.random.normal(jax.random.fold_in(key, 22), small_shape, jnp.float32)
    noise = 0.45 * jax.random.normal(jax.random.fold_in(key, 23), full_shape, jnp.float32)
    common = first * jnp.cos(phase) + second * jnp.sin(phase)
    return jnp.clip(common + noise, -6.0, 6.0).astype(jnp.bfloat16)


def draw_control(key, part):
    local = jnp.arange(NY, dtype=jnp.int32) % ROWS_DEV
    depth = jnp.minimum(local, ROWS_DEV - 1 - local)
    far_rows = ((depth == 2) | (depth == 3))[None, :, None]
    shape = (C, NY, NX)
    signs = jnp.where(jax.random.bernoulli(jax.random.fold_in(key, 31), 0.5, shape), 1.0, -1.0)
    base = jnp.clip(jax.random.normal(jax.random.fold_in(key, 32), shape, jnp.float32), -4.0, 4.0)
    magnitude = jax.random.uniform(jax.random.fold_in(key, 33), shape, jnp.float32, 3.0, 6.0)
    return jnp.where(far_rows, signs * magnitude, base)


def with_ends(drawn, rng, low, high):
    index_at = [jax.random.randint(jax.random.fold_in(rng, axis), (), 0, length) for axis, length in enumerate(drawn.shape)]
    main_axis = drawn.shape.index(max(drawn.shape))
    beside = index_at[:main_axis] + [(index_at[main_axis] + 1) % drawn.shape[main_axis]] + index_at[main_axis + 1:]
    return drawn.at[tuple(index_at)].set(low).at[tuple(beside)].set(high)


def setup_inputs(seed: int = 0) -> dict:
    keys = jax.random.split(jax.random.key(seed), 9)
    return {
        "members": draw_members(jax.random.fold_in(keys[8], 71), 0),
        "control": draw_control(jax.random.fold_in(keys[8], 71), 0),
        "hybrid_weight": jnp.clip(jax.random.uniform(keys[2], (C,), jnp.float32, 0.2, 0.6), 0.2, 0.6),
        "member_weights": with_ends(jax.random.randint(keys[3], (MEMBERS,), 1, 9), jax.random.fold_in(keys[3], 1), 1, 8).astype(jnp.int32),
        "source_device": draw_source_device(jax.random.fold_in(keys[8], 71), 0),
        "source_row": draw_source_row(jax.random.fold_in(keys[8], 71), 0),
        "column_source": draw_column_source(jax.random.fold_in(keys[8], 71), 0),
        "column_code": with_ends(jax.random.randint(keys[7], (NY, FX), 0, 17), jax.random.fold_in(keys[7], 1), 0, 16).astype(jnp.int32),
    }


DIFFUSE = 0.2


def sweep_field(field):
    widths = [(0, 0)] * (field.ndim - 2) + [(1, 1), (1, 1)]
    padded = jnp.pad(field, widths)
    laplace = padded[..., 2:, 1:-1] + padded[..., :-2, 1:-1] + padded[..., 1:-1, 2:] + padded[..., 1:-1, :-2] - 4.0 * field
    return field + DIFFUSE * laplace


def localize(field):
    for repeat in range(SWEEPS):
        field = sweep_field(field)
    return field


def reference(members, control, hybrid_weight, member_weights, source_device, source_row, column_source, column_code):
    weight_codes = member_weights.astype(jnp.float32)
    member_share = weight_codes / jnp.sum(weight_codes)

    def add_member(total, item):
        member, weight = item
        states = member.astype(jnp.float32)
        smooth = localize(states * control)
        return total + weight * (states * smooth), None

    ensemble, unused = lax.scan(add_member, jnp.zeros(control.shape, jnp.float32), (members, member_share))
    static = localize(control)
    blend = hybrid_weight[:, None, None]
    increment = (1.0 - blend) * ensemble + blend * static
    extended = jnp.concatenate([increment, jnp.zeros((control.shape[0], 1, control.shape[2]), jnp.float32)], axis=1)
    global_rows = (source_device[:, 0] * ROWS_DEV + source_row).astype(jnp.int32)
    lower = jnp.take(extended, global_rows, axis=1)
    upper = jnp.take(extended, (global_rows + 1).astype(jnp.int32), axis=1)
    fine_rows = jnp.stack([0.75 * lower + 0.25 * upper, 0.25 * lower + 0.75 * upper], axis=2)
    full_shape = (fine_rows.shape[0], fine_rows.shape[1], 2, column_source.shape[1])
    left_index = jnp.broadcast_to(column_source[None, :, None, :], full_shape).astype(jnp.int32)
    right_index = (left_index + 1).astype(jnp.int32)
    left_value = jnp.take_along_axis(fine_rows, left_index, axis=3)
    right_value = jnp.take_along_axis(fine_rows, right_index, axis=3)
    right_weight = (column_code.astype(jnp.float32) / 16.0)[None, :, None, :]
    fine = (1.0 - right_weight) * left_value + right_weight * right_value
    return jnp.transpose(fine, (1, 0, 2, 3))
```

```python
import functools

import jax
import jax.numpy as jnp
from jax import lax
from jax.experimental import pallas as pl
from jax.experimental.pallas import tpu as pltpu
from jax.sharding import PartitionSpec as P

SWEEPS = 4
DIFFUSE = 0.2
SCALE = DIFFUSE**SWEEPS
REACH = SWEEPS // 2
LANES = 128
MESH = pl.DeviceIdType.MESH


def beside(x):
    width = x.shape[-1]
    lane = lax.broadcasted_iota(jnp.int32, x.shape, x.ndim - 1)
    left = jnp.where(lane == 0, 0.0, pltpu.roll(x, 1, x.ndim - 1))
    right = jnp.where(lane == width - 1, 0.0, pltpu.roll(x, width - 1, x.ndim - 1))
    return left + right


def apply_kernel(
    spaces,
    slots,
    members,
    control,
    edges,
    own,
    weight,
    blend,
    request,
    arrived,
    perm,
    states,
    stage_up,
    stage_down,
    recv_low,
    recv_high,
    ctrl_low,
    ctrl_high,
    ext_x,
    buf_a,
    buf_b,
    stat_a,
    stat_b,
    acc,
    red,
    ext,
    from_low,
    from_high,
    fin,
    asked,
    outgoing,
    load_sem,
    up_send,
    up_recv,
    down_send,
    down_recv,
    edge_send,
    edge_recv,
    ask_send,
    ask_recv,
    red_send,
    red_recv,
    fix_send,
    fix_recv,
    out_send,
    out_recv,
    own_sem,
):
    me = lax.axis_index("space")
    slot = lax.axis_index("member")
    count, chans, rows, width = members.shape
    own_chans = chans // slots
    capacity = request.shape[1]
    has_low = me > 0
    has_high = me < spaces - 1
    low_mask = jnp.where(has_low, 1.0, 0.0).astype(jnp.float32)
    high_mask = jnp.where(has_high, 1.0, 0.0).astype(jnp.float32)
    low, high = {"space": me - 1}, {"space": me + 1}

    def load(group):
        owner = lax.rem(slot + 1 + group, slots)
        first = pl.multiple_of(owner * own_chans, own_chans)
        return pltpu.make_async_copy(
            members.at[:, pl.ds(first, own_chans)], states.at[group], load_sem.at[group]
        )

    for group in range(slots):
        load(group).start()

    barrier = pltpu.get_barrier_semaphore()
    for step in range(1, spaces):
        pl.semaphore_signal(
            barrier, inc=1, device_id={"space": lax.rem(me + step, spaces)}, device_id_type=MESH
        )
    for step in range(1, slots):
        pl.semaphore_signal(
            barrier, inc=1, device_id={"member": lax.rem(slot + step, slots)}, device_id_type=MESH
        )

    place = lax.broadcasted_iota(jnp.int32, perm.shape, 0)
    source = lax.broadcasted_iota(jnp.int32, perm.shape, 1)
    wanted = lax.rem(place, count) * rows + place // count
    perm[...] = jnp.where(source == wanted, 1.0, 0.0).astype(jnp.bfloat16)

    pl.semaphore_wait(barrier, spaces + slots - 2)

    def remote(src, dst, send, recv, device):
        return pltpu.make_async_remote_copy(
            src_ref=src,
            dst_ref=dst,
            send_sem=send,
            recv_sem=recv,
            device_id=device,
            device_id_type=MESH,
        )

    def edge_up():
        return remote(
            edges.at[pl.ds(0, REACH)], ctrl_high, edge_send.at[0], edge_recv.at[0], low
        )

    def edge_down():
        return remote(
            edges.at[pl.ds(REACH, REACH)], ctrl_low, edge_send.at[1], edge_recv.at[1], high
        )

    def halo_up(turn):
        return remote(
            stage_up.at[turn], recv_high.at[turn], up_send.at[turn], up_recv.at[turn], low
        )

    def halo_down(turn):
        return remote(
            stage_down.at[turn], recv_low.at[turn], down_send.at[turn], down_recv.at[turn], high
        )

    def ask(step):
        target = lax.rem(me + step, spaces)
        return remote(
            request.at[target],
            asked.at[step - 1],
            ask_send.at[step - 1],
            ask_recv.at[step - 1],
            {"space": target},
        )

    @pl.when(has_low)
    def _():
        edge_up().start()

    @pl.when(has_high)
    def _():
        edge_down().start()

    span = REACH * count
    for group in range(slots):
        load(group).wait()

        def send_edges(index, carry, group=group):
            turn = group * own_chans + index
            flat = states[group, :, index].reshape(count * rows, width)
            picks = jnp.concatenate(
                [perm[pl.ds(0, span), :], perm[pl.ds((rows - REACH) * count, span), :]], axis=0
            )
            both = jnp.dot(picks, flat, preferred_element_type=jnp.float32)
            stage_up[turn] = both[:span]
            stage_down[turn] = both[span:]

            @pl.when(has_low)
            def _():
                halo_up(turn).start()

            @pl.when(has_high)
            def _():
                halo_down(turn).start()

            return carry

        lax.fori_loop(0, own_chans, send_edges, 0)

    for step in range(1, spaces):
        ask(step).start()

    @pl.when(jnp.logical_not(has_low))
    def _():
        recv_low[...] = jnp.zeros_like(recv_low)
        ctrl_low[...] = jnp.zeros_like(ctrl_low)
        from_low[...] = jnp.zeros_like(from_low)

    @pl.when(jnp.logical_not(has_high))
    def _():
        recv_high[...] = jnp.zeros_like(recv_high)
        ctrl_high[...] = jnp.zeros_like(ctrl_high)
        from_high[...] = jnp.zeros_like(from_high)

    def swept(ref, at):
        middle = ref[at]
        return ref[at - 1] + ref[at + 1] + (middle + beside(middle))

    def masked(value, row):
        if row < 0:
            return value * low_mask
        if row >= rows:
            return value * high_mask
        return value

    stat_a[...] = jnp.zeros_like(stat_a)
    stat_b[...] = jnp.zeros_like(stat_b)
    margin = SWEEPS + 1
    for row in range(rows):
        stat_a[margin + row] = own[row]
    here, there = stat_a, stat_b
    for sweep in range(1, SWEEPS + 1):
        for row in range(-sweep, rows + sweep):
            there[margin + row] = masked(swept(here, margin + row), row)
        here, there = there, here
    static = here

    buf_a[...] = jnp.zeros_like(buf_a)
    buf_b[...] = jnp.zeros_like(buf_b)
    base = REACH + 2

    @pl.when(has_low)
    def _():
        edge_down().wait_recv()

    @pl.when(has_high)
    def _():
        edge_up().wait_recv()

    def give(group):
        return remote(
            acc.at[group],
            red.at[group],
            red_send.at[group],
            red_recv.at[group],
            {"member": lax.rem(slot + 1 + group, slots)},
        )

    for group in range(slots):
        owner = lax.rem(slot + 1 + group, slots)

        def one_channel(index, carry, group=group, owner=owner):
            turn = group * own_chans + index
            chan = owner * own_chans + index
            flat = states[group, :, index].reshape(count * rows, width)
            ext_x[pl.ds(REACH * count, rows * count), :] = jnp.dot(
                perm[...], flat, preferred_element_type=jnp.float32
            )

            @pl.when(has_low)
            def _():
                halo_down(turn).wait_recv()

            @pl.when(has_high)
            def _():
                halo_up(turn).wait_recv()

            ext_x[pl.ds(0, span), :] = recv_low[turn]
            ext_x[pl.ds((rows + REACH) * count, span), :] = recv_high[turn]

            def state(row):
                return ext_x[pl.ds((row + REACH) * count, count), :]

            for row in range(-REACH, rows + REACH):
                if row < 0:
                    line = ctrl_low[row + REACH, pl.ds(chan, 1), :]
                elif row >= rows:
                    line = ctrl_high[row - rows, pl.ds(chan, 1), :]
                else:
                    line = control[chan, pl.ds(row, 1), :]
                buf_a[base + row] = state(row) * line

            def collect(row, value):
                total = jnp.sum(state(row) * value * weight[...], axis=0, keepdims=True)
                acc[group, row + REACH, pl.ds(index, 1), :] = total

            for outer, inner, away in ((-1, 2, 1), (rows, rows - 3, -1)):
                near = buf_a[base + inner]
                far = buf_a[base + inner + away]
                collect(outer, SWEEPS * (near + beside(near)) + far)
                collect(outer - away, near)

            for row in range(-3, rows + 3):
                buf_b[base + row] = masked(swept(buf_a, base + row), row)
            for row in range(-2, rows + 2):
                buf_a[base + row] = masked(swept(buf_b, base + row), row)
            for row in range(-1, rows + 1):
                buf_b[base + row] = masked(swept(buf_a, base + row), row)
            for row in range(rows):
                collect(row, swept(buf_b, base + row))
            return carry

        lax.fori_loop(0, own_chans, one_channel, 0)
        if group < slots - 1:
            give(group).start()

    for group in range(slots - 1):
        give(group).wait_recv()
    share = blend[...]
    for row in range(-SWEEPS, rows + SWEEPS):
        value = (share * SCALE) * static[margin + row]
        if -REACH <= row < rows + REACH:
            total = acc[slots - 1, row + REACH]
            for group in range(slots - 1):
                total = total + red[group, row + REACH]
            value = value + (1.0 - share) * total
        ext[row + SWEEPS] = value

    def fix_up():
        return remote(
            ext.at[pl.ds(0, SWEEPS + 1)], from_high, fix_send.at[0], fix_recv.at[0], low
        )

    def fix_down():
        return remote(
            ext.at[pl.ds(rows + SWEEPS, SWEEPS)], from_low, fix_send.at[1], fix_recv.at[1], high
        )

    @pl.when(has_low)
    def _():
        fix_up().start()

    @pl.when(has_high)
    def _():
        fix_down().start()

    @pl.when(has_low)
    def _():
        fix_down().wait_recv()

    @pl.when(has_high)
    def _():
        fix_up().wait_recv()

    for row in range(rows + 1):
        value = ext[row + SWEEPS]
        if row < SWEEPS:
            value = value + from_low[row]
        if row >= rows - SWEEPS:
            value = value + from_high[row - rows + SWEEPS]
        fin[row] = value

    def answer(step):
        target = lax.rem(me + spaces - step, spaces)
        return remote(
            outgoing.at[step],
            arrived.at[me],
            out_send.at[step - 1],
            out_recv.at[step - 1],
            {"space": target},
        )

    def keep():
        return pltpu.make_async_copy(outgoing.at[0], arrived.at[me], own_sem)

    def fill(step, wants):
        for place in range(capacity):
            line = wants[place]
            line = jnp.concatenate([line] * (width // LANES), axis=1)
            line = jnp.broadcast_to(line, (own_chans, width))
            lower, upper = fin[0], fin[1]
            for row in range(1, rows):
                hit = line == row
                lower = jnp.where(hit, fin[row], lower)
                upper = jnp.where(hit, fin[row + 1], upper)
            outgoing[step, place, 0] = lower
            outgoing[step, place, 1] = upper

    for step in range(1, spaces):
        ask(step).wait_recv()
    for step in range(1, spaces):
        fill(step, [asked[step - 1, pl.ds(place, 1), :] for place in range(capacity)])
        answer(step).start()
    fill(0, [request[me, pl.ds(place, 1), :] for place in range(capacity)])
    keep().start()

    for step in range(1, spaces):
        answer(step).wait_recv()
    keep().wait()
    for step in range(1, spaces):
        answer(step).wait_send()
        ask(step).wait_send()
    for group in range(slots - 1):
        give(group).wait_send()

    @pl.when(has_low)
    def _():
        edge_up().wait_send()
        fix_up().wait_send()

    @pl.when(has_high)
    def _():
        edge_down().wait_send()
        fix_down().wait_send()

    def drain(turn, carry):
        @pl.when(has_low)
        def _():
            halo_up(turn).wait_send()

        @pl.when(has_high)
        def _():
            halo_down(turn).wait_send()

        return carry

    lax.fori_loop(0, chans, drain, 0)


def regrid_kernel(slot_index, column_source, column_code, arrived, out):
    blocks, _, fine = column_source.shape
    chans, width = arrived.shape[2], arrived.shape[3]
    tiles = width // LANES

    def one_block(block, carry):
        at = slot_index[block]
        lower = arrived[at, 0]
        upper = arrived[at, 1]
        pair = (0.75 * lower + 0.25 * upper, 0.25 * lower + 0.75 * upper)
        for tile in range(fine // LANES):
            columns = pl.ds(tile * LANES, LANES)
            left = jnp.broadcast_to(column_source[block, :, columns], (chans, LANES))
            code = jnp.broadcast_to(column_code[block, :, columns], (chans, LANES))
            right_weight = code.astype(jnp.float32) / 16.0
            first = max(0, (tile * LANES - 1) // 2 - 2) // LANES
            last = min(width - 1, ((tile + 1) * LANES - 2) // 2 + 3) // LANES

            def value(field, index):
                found = None
                for part in range(first, min(last, tiles - 1) + 1):
                    piece = field[:, part * LANES : (part + 1) * LANES]
                    got = jnp.take_along_axis(piece, lax.rem(index, LANES), axis=1)
                    if found is None:
                        found = got
                    else:
                        found = jnp.where(index >= part * LANES, got, found)
                return found

            for half in range(2):
                out[block, :, half, columns] = (1.0 - right_weight) * value(
                    pair[half], left
                ) + right_weight * value(pair[half], left + 1)
        return carry

    lax.fori_loop(0, blocks, one_block, 0)


def per_device(
    members,
    control,
    hybrid_weight,
    member_weights,
    source_device,
    source_row,
    column_source,
    column_code,
):
    count, chans, rows, width = members.shape
    spaces, slots = lax.axis_size("space"), lax.axis_size("member")
    slot = lax.axis_index("member")
    own_chans = chans // slots
    capacity = max(2, 2 * rows // spaces)
    f32 = jnp.float32

    codes = member_weights.astype(f32)
    share = lax.dynamic_slice_in_dim(codes, slot * count, count) / jnp.sum(codes)
    weight = jnp.broadcast_to((share * SCALE)[:, None], (count, width))
    blend = lax.dynamic_slice_in_dim(hybrid_weight, slot * own_chans, own_chans)
    blend = jnp.broadcast_to(blend[:, None], (own_chans, width))
    edges = jnp.concatenate([control[:, :REACH], control[:, rows - REACH :]], axis=1)
    edges = jnp.swapaxes(edges, 0, 1)
    own = lax.dynamic_slice_in_dim(control, slot * own_chans, own_chans, 0)
    own = jnp.swapaxes(own, 0, 1)

    source = source_device[:, 0]
    order = jnp.arange(rows, dtype=jnp.int32)
    same = (source[:, None] == source[None, :]) & (order[None, :] < order[:, None])
    slot_index = source * capacity + jnp.sum(same.astype(jnp.int32), axis=1)
    matches = slot_index[None, :] == jnp.arange(spaces * capacity, dtype=jnp.int32)[:, None]
    request = jnp.sum(jnp.where(matches, source_row[None, :], 0), axis=1)
    request = jnp.broadcast_to(
        request.reshape(spaces, capacity)[:, :, None], (spaces, capacity, LANES)
    )

    vmem = pl.BlockSpec(memory_space=pltpu.VMEM)
    anywhere = pl.BlockSpec(memory_space=pl.ANY)
    dma = pltpu.SemaphoreType.DMA
    halo = pltpu.VMEM((chans, REACH * count, width), f32)
    line = pltpu.VMEM((REACH, chans, width), f32)
    ext_rows = rows + 2 * REACH
    arrived = pl.pallas_call(
        functools.partial(apply_kernel, spaces, slots),
        out_shape=jax.ShapeDtypeStruct((spaces, capacity, 2, own_chans, width), f32),
        in_specs=[anywhere] + [vmem] * 6,
        out_specs=anywhere,
        scratch_shapes=[
            pltpu.VMEM((rows * count, rows * count), jnp.bfloat16),
            pltpu.VMEM((slots, count, own_chans, rows, width), jnp.bfloat16),
            halo,
            halo,
            halo,
            halo,
            line,
            line,
            pltpu.VMEM((ext_rows * count, width), f32),
            pltpu.VMEM((rows + 2 * (REACH + 2), count, width), f32),
            pltpu.VMEM((rows + 2 * (REACH + 2), count, width), f32),
            pltpu.VMEM((rows + 2 * (SWEEPS + 1), own_chans, width), f32),
            pltpu.VMEM((rows + 2 * (SWEEPS + 1), own_chans, width), f32),
            pltpu.VMEM((slots, ext_rows, own_chans, width), f32),
            pltpu.VMEM((slots - 1, ext_rows, own_chans, width), f32),
            pltpu.VMEM((rows + 2 * SWEEPS, own_chans, width), f32),
            pltpu.VMEM((SWEEPS, own_chans, width), f32),
            pltpu.VMEM((SWEEPS + 1, own_chans, width), f32),
            pltpu.VMEM((rows + 1, own_chans, width), f32),
            pltpu.VMEM((spaces - 1, capacity, LANES), jnp.int32),
            pltpu.VMEM((spaces, capacity, 2, own_chans, width), f32),
            dma((slots,)),
            dma((chans,)),
            dma((chans,)),
            dma((chans,)),
            dma((chans,)),
            dma((2,)),
            dma((2,)),
            dma((spaces - 1,)),
            dma((spaces - 1,)),
            dma((slots - 1,)),
            dma((slots - 1,)),
            dma((2,)),
            dma((2,)),
            dma((spaces - 1,)),
            dma((spaces - 1,)),
            dma,
        ],
        compiler_params=pltpu.CompilerParams(
            collective_id=0, has_side_effects=True, vmem_limit_bytes=48 * 2**20
        ),
        name="covariance_apply",
    )(members, control, edges, own, weight, blend, request)

    arrived = arrived.reshape(spaces * capacity, 2, own_chans, width)
    return pl.pallas_call(
        regrid_kernel,
        out_shape=jax.ShapeDtypeStruct((rows, own_chans, 2, column_source.shape[1]), f32),
        in_specs=[pl.BlockSpec(memory_space=pltpu.SMEM)] + [vmem] * 3,
        out_specs=vmem,
        compiler_params=pltpu.CompilerParams(vmem_limit_bytes=32 * 2**20),
        name="regrid",
    )(slot_index, column_source[:, None], column_code[:, None], arrived)


def solution(mesh):
    placed = (
        P("member", None, "space", None),
        P(None, "space", None),
        P(),
        P(),
        P("space", None),
        P("space"),
        P("space", None),
        P("space", None),
    )
    return jax.shard_map(
        per_device,
        mesh=mesh,
        in_specs=placed,
        out_specs=P("space", "member", None, None),
        check_vma=False,
    )
```

```python
import functools

import jax
import jax.numpy as jnp
from jax import lax
from jax.experimental import pallas as pl
from jax.experimental.pallas import tpu as pltpu
from jax.sharding import PartitionSpec as P

SWEEPS = 4
DIFFUSE = 0.2
SCALE = DIFFUSE**SWEEPS
REACH = SWEEPS // 2
LANES = 128
GROUP = 8
PARTS = 2
AHEAD = 1
MESH = pl.DeviceIdType.MESH


def beside(x):
    width = x.shape[-1]
    lane = lax.broadcasted_iota(jnp.int32, x.shape, x.ndim - 1)
    left = jnp.where(lane == 0, 0.0, pltpu.roll(x, 1, x.ndim - 1))
    right = jnp.where(lane == width - 1, 0.0, pltpu.roll(x, width - 1, x.ndim - 1))
    return left + right


def ranked(source_device, capacity):
    blocks = source_device.shape[0]
    devices = [source_device[block] for block in range(blocks)]
    found = []
    for block in range(blocks):
        rank = jnp.int32(0)
        for earlier in range(block):
            rank = rank + (devices[earlier] == devices[block]).astype(jnp.int32)
        found.append(devices[block] * capacity + rank)
    return found


def apply_kernel(
    spaces,
    slots,
    capacity,
    members,
    control_hbm,
    hybrid_weight,
    member_weights,
    source_device,
    source_row,
    arrived,
    perm,
    states,
    control,
    weight,
    blend,
    request,
    edges,
    stage_up,
    stage_down,
    recv_low,
    recv_high,
    ctrl_low,
    ctrl_high,
    ext_x,
    buf_a,
    buf_b,
    stat_a,
    stat_b,
    acc,
    red,
    ext,
    from_low,
    from_high,
    fin,
    asked,
    outgoing,
    load_sem,
    ctrl_sem,
    up_send,
    up_recv,
    down_send,
    down_recv,
    edge_send,
    edge_recv,
    ask_send,
    ask_recv,
    red_send,
    red_recv,
    fix_send,
    fix_recv,
    out_send,
    out_recv,
    own_sem,
):
    me = lax.axis_index("space")
    slot = lax.axis_index("member")
    count, chans, rows, width = members.shape
    own_chans = chans // slots
    parts, some = acc.shape[0], acc.shape[3]
    chunks = parts * slots
    has_low = me > 0
    has_high = me < spaces - 1
    low_mask = jnp.where(has_low, 1.0, 0.0).astype(jnp.float32)
    high_mask = jnp.where(has_high, 1.0, 0.0).astype(jnp.float32)
    low, high = {"space": me - 1}, {"space": me + 1}

    def first_chan(chunk):
        owner = lax.rem(slot + 1 + chunk % slots, slots)
        return owner * own_chans + (chunk // slots) * some

    def load(chunk):
        return pltpu.make_async_copy(
            members.at[:, pl.ds(first_chan(chunk), some)], states.at[chunk], load_sem.at[chunk]
        )

    def load_control():
        return pltpu.make_async_copy(control_hbm, control, ctrl_sem)

    load_control().start()
    for chunk in range(chunks):
        load(chunk).start()

    barrier = pltpu.get_barrier_semaphore()
    for step in range(1, spaces):
        pl.semaphore_signal(
            barrier, inc=1, device_id={"space": lax.rem(me + step, spaces)}, device_id_type=MESH
        )
    for step in range(1, slots):
        pl.semaphore_signal(
            barrier, inc=1, device_id={"member": lax.rem(slot + step, slots)}, device_id_type=MESH
        )

    place = lax.broadcasted_iota(jnp.int32, perm.shape, 0)
    source = lax.broadcasted_iota(jnp.int32, perm.shape, 1)
    wanted = lax.rem(place, count) * rows + place // count
    perm[...] = jnp.where(source == wanted, 1.0, 0.0).astype(jnp.bfloat16)

    load_control().wait()
    edges[0] = control[:, :REACH, :]
    edges[1] = control[:, rows - REACH :, :]
    pl.semaphore_wait(barrier, spaces + slots - 2)

    def remote(src, dst, send, recv, device):
        return pltpu.make_async_remote_copy(
            src_ref=src,
            dst_ref=dst,
            send_sem=send,
            recv_sem=recv,
            device_id=device,
            device_id_type=MESH,
        )

    def edge_up():
        return remote(edges.at[0], ctrl_high, edge_send.at[0], edge_recv.at[0], low)

    def edge_down():
        return remote(edges.at[1], ctrl_low, edge_send.at[1], edge_recv.at[1], high)

    def halo_up(turn):
        return remote(
            stage_up.at[turn], recv_high.at[turn], up_send.at[turn], up_recv.at[turn], low
        )

    def halo_down(turn):
        return remote(
            stage_down.at[turn], recv_low.at[turn], down_send.at[turn], down_recv.at[turn], high
        )

    def ask(step):
        target = lax.rem(me + step, spaces)
        return remote(
            request.at[target],
            asked.at[step - 1],
            ask_send.at[step - 1],
            ask_recv.at[step - 1],
            {"space": target},
        )

    @pl.when(has_low)
    def _():
        edge_up().start()

    @pl.when(has_high)
    def _():
        edge_down().start()

    span = REACH * count

    def send_edges(chunk, index):
        turn = chunk * some + index
        flat = states[chunk, :, index].reshape(count * rows, width)
        picks = jnp.concatenate(
            [perm[pl.ds(0, span), :], perm[pl.ds((rows - REACH) * count, span), :]], axis=0
        )
        both = jnp.dot(picks, flat, preferred_element_type=jnp.float32)
        stage_up[turn] = both[:span]
        stage_down[turn] = both[span:]

        @pl.when(has_low)
        def _():
            halo_up(turn).start()

        @pl.when(has_high)
        def _():
            halo_down(turn).start()

    for chunk in range(AHEAD):
        load(chunk).wait()

        def ahead(index, carry, chunk=chunk):
            send_edges(chunk, index)
            return carry

        lax.fori_loop(0, some, ahead, 0)

    shape = request.shape
    number = lax.broadcasted_iota(jnp.int32, shape, 0) * capacity
    number = number + lax.broadcasted_iota(jnp.int32, shape, 1)
    needs = jnp.zeros(shape, jnp.int32)
    for block, at in enumerate(ranked(source_device, capacity)):
        needs = jnp.where(number == at, source_row[block], needs)
    request[...] = needs
    for step in range(1, spaces):
        ask(step).start()

    total = lax.fori_loop(
        0,
        member_weights.shape[0],
        lambda index, so_far: so_far + member_weights[index],
        jnp.int32(0),
    )
    which = lax.broadcasted_iota(jnp.int32, weight.shape, 0)
    value = jnp.zeros(weight.shape, jnp.float32)
    for index in range(count):
        code = member_weights[slot * count + index].astype(jnp.float32)
        value = jnp.where(which == index, code, value)
    weight[...] = value / jnp.full(weight.shape, total.astype(jnp.float32)) * SCALE
    which = lax.broadcasted_iota(jnp.int32, blend.shape, 0)
    value = jnp.zeros(blend.shape, jnp.float32)
    for index in range(own_chans):
        value = jnp.where(which == index, hybrid_weight[slot * own_chans + index], value)
    blend[...] = value

    @pl.when(jnp.logical_not(has_low))
    def _():
        recv_low[...] = jnp.zeros_like(recv_low)
        ctrl_low[...] = jnp.zeros_like(ctrl_low)
        from_low[...] = jnp.zeros_like(from_low)

    @pl.when(jnp.logical_not(has_high))
    def _():
        recv_high[...] = jnp.zeros_like(recv_high)
        ctrl_high[...] = jnp.zeros_like(ctrl_high)
        from_high[...] = jnp.zeros_like(from_high)

    def swept(ref, at):
        middle = ref[at]
        return ref[at - 1] + ref[at + 1] + (middle + beside(middle))

    def masked(value, row):
        if row < 0:
            return value * low_mask
        if row >= rows:
            return value * high_mask
        return value

    stat_a[...] = jnp.zeros_like(stat_a)
    stat_b[...] = jnp.zeros_like(stat_b)
    margin = SWEEPS + 1
    for index in range(own_chans):
        field = control[slot * own_chans + index]
        for row in range(rows):
            stat_a[margin + row, pl.ds(index, 1), :] = field[row : row + 1]
    here, there = stat_a, stat_b
    for sweep in range(1, SWEEPS + 1):
        for row in range(-sweep, rows + sweep):
            there[margin + row] = masked(swept(here, margin + row), row)
        here, there = there, here
    static = here

    buf_a[...] = jnp.zeros_like(buf_a)
    buf_b[...] = jnp.zeros_like(buf_b)
    base = REACH + 2

    @pl.when(has_low)
    def _():
        edge_down().wait_recv()

    @pl.when(has_high)
    def _():
        edge_up().wait_recv()

    def give(part, group):
        return remote(
            acc.at[part, group],
            red.at[part, group],
            red_send.at[part, group],
            red_recv.at[part, group],
            {"member": lax.rem(slot + 1 + group, slots)},
        )

    def fix_up(part):
        return remote(
            ext.at[part, pl.ds(0, SWEEPS + 1)],
            from_high.at[part],
            fix_send.at[part, 0],
            fix_recv.at[part, 0],
            low,
        )

    def fix_down(part):
        return remote(
            ext.at[part, pl.ds(rows + SWEEPS, SWEEPS)],
            from_low.at[part],
            fix_send.at[part, 1],
            fix_recv.at[part, 1],
            high,
        )

    def answer(part, step):
        target = lax.rem(me + spaces - step, spaces)
        return remote(
            outgoing.at[part, step],
            arrived.at[part, me],
            out_send.at[part, step - 1],
            out_recv.at[part, step - 1],
            {"space": target},
        )

    def keep(part):
        return pltpu.make_async_copy(
            outgoing.at[part, 0], arrived.at[part, me], own_sem.at[part]
        )

    def combine(part):
        for group in range(slots - 1):
            give(part, group).wait_recv()
        mine = slice(part * some, (part + 1) * some)
        share = blend[mine, :]
        for row in range(-SWEEPS, rows + SWEEPS):
            value = (share * SCALE) * static[margin + row, mine, :]
            if -REACH <= row < rows + REACH:
                total = acc[part, slots - 1, row + REACH]
                for group in range(slots - 1):
                    total = total + red[part, group, row + REACH]
                value = value + (1.0 - share) * total
            ext[part, row + SWEEPS] = value

        @pl.when(has_low)
        def _():
            fix_up(part).start()

        @pl.when(has_high)
        def _():
            fix_down(part).start()

    def fill(part, step, wants):
        for place in range(capacity):
            line = jnp.concatenate([wants[place]] * (width // LANES), axis=1)
            line = jnp.broadcast_to(line, (some, width))
            lower, upper = fin[part, 0], fin[part, 1]
            for row in range(1, rows):
                hit = line == row
                lower = jnp.where(hit, fin[part, row], lower)
                upper = jnp.where(hit, fin[part, row + 1], upper)
            outgoing[part, step, place, 0] = lower
            outgoing[part, step, place, 1] = upper

    def serve(part):
        @pl.when(has_low)
        def _():
            fix_down(part).wait_recv()

        @pl.when(has_high)
        def _():
            fix_up(part).wait_recv()

        for row in range(rows + 1):
            value = ext[part, row + SWEEPS]
            if row < SWEEPS:
                value = value + from_low[part, row]
            if row >= rows - SWEEPS:
                value = value + from_high[part, row - rows + SWEEPS]
            fin[part, row] = value
        if part == 0:
            for step in range(1, spaces):
                ask(step).wait_recv()
        for step in sorted(range(1, spaces), key=lambda step: -min(step, spaces - step)):
            fill(part, step, [asked[step - 1, pl.ds(p, 1), :] for p in range(capacity)])
            answer(part, step).start()
        fill(part, 0, [request[me, pl.ds(p, 1), :] for p in range(capacity)])
        keep(part).start()

    for chunk in range(chunks):
        part, group = chunk // slots, chunk % slots
        if chunk + AHEAD < chunks:
            load(chunk + AHEAD).wait()

        def one_channel(index, carry, chunk=chunk, part=part, group=group):
            turn = chunk * some + index
            chan = first_chan(chunk) + index
            if chunk + AHEAD < chunks:
                send_edges(chunk + AHEAD, index)
            flat = states[chunk, :, index].reshape(count * rows, width)
            ext_x[pl.ds(span, rows * count), :] = jnp.dot(
                perm[...], flat, preferred_element_type=jnp.float32
            )

            @pl.when(has_low)
            def _():
                halo_down(turn).wait_recv()

            @pl.when(has_high)
            def _():
                halo_up(turn).wait_recv()

            ext_x[pl.ds(0, span), :] = recv_low[turn]
            ext_x[pl.ds((rows + REACH) * count, span), :] = recv_high[turn]

            def state(row):
                return ext_x[pl.ds((row + REACH) * count, count), :]

            for row in range(-REACH, rows + REACH):
                if row < 0:
                    line = ctrl_low[chan, pl.ds(row + REACH, 1), :]
                elif row >= rows:
                    line = ctrl_high[chan, pl.ds(row - rows, 1), :]
                else:
                    line = control[chan, pl.ds(row, 1), :]
                buf_a[base + row] = state(row) * line

            def collect(row, value):
                total = jnp.sum(state(row) * value * weight[...], axis=0, keepdims=True)
                acc[part, group, row + REACH, pl.ds(index, 1), :] = total

            for outer, inner, away in ((-1, 2, 1), (rows, rows - 3, -1)):
                near = buf_a[base + inner]
                far = buf_a[base + inner + away]
                collect(outer, SWEEPS * (near + beside(near)) + far)
                collect(outer - away, near)

            for row in range(-3, rows + 3):
                buf_b[base + row] = masked(swept(buf_a, base + row), row)
            for row in range(-2, rows + 2):
                buf_a[base + row] = masked(swept(buf_b, base + row), row)
            for row in range(-1, rows + 1):
                buf_b[base + row] = masked(swept(buf_a, base + row), row)
            for row in range(rows):
                collect(row, swept(buf_b, base + row))
            return carry

        lax.fori_loop(0, some, one_channel, 0)
        if group < slots - 1:
            give(part, group).start()
        else:
            combine(part)
        if group == 0 and part > 0:
            serve(part - 1)

    serve(parts - 1)

    for part in range(parts):
        for step in range(1, spaces):
            answer(part, step).wait_recv()
        keep(part).wait()
        for step in range(1, spaces):
            answer(part, step).wait_send()
        for group in range(slots - 1):
            give(part, group).wait_send()

        @pl.when(has_low)
        def _():
            fix_up(part).wait_send()

        @pl.when(has_high)
        def _():
            fix_down(part).wait_send()

    for step in range(1, spaces):
        ask(step).wait_send()

    @pl.when(has_low)
    def _():
        edge_up().wait_send()

    @pl.when(has_high)
    def _():
        edge_down().wait_send()

    def drain(turn, carry):
        @pl.when(has_low)
        def _():
            halo_up(turn).wait_send()

        @pl.when(has_high)
        def _():
            halo_down(turn).wait_send()

        return carry

    lax.fori_loop(0, chans, drain, 0)


def regrid_kernel(capacity, source_device, column_source, column_code, arrived, out, slot_index):
    blocks, fine = column_source.shape
    parts, some, width = arrived.shape[0], arrived.shape[3], arrived.shape[4]
    chans = parts * some
    tiles = width // LANES
    for block, at in enumerate(ranked(source_device, capacity)):
        slot_index[block] = at

    def one_group(group, carry):
        lines = pl.ds(pl.multiple_of(group * GROUP, GROUP), GROUP)
        sources = column_source[lines, :]
        codes = column_code[lines, :].astype(jnp.float32) / 16.0
        for inner in range(GROUP):
            block = group * GROUP + inner
            at = slot_index[block]
            lower = jnp.concatenate([arrived[part, at, 0] for part in range(parts)], axis=0)
            upper = jnp.concatenate([arrived[part, at, 1] for part in range(parts)], axis=0)
            pair = (0.75 * lower + 0.25 * upper, 0.25 * lower + 0.75 * upper)
            for tile in range(fine // LANES):
                columns = slice(tile * LANES, (tile + 1) * LANES)
                spread = (chans, LANES)
                left = jnp.broadcast_to(sources[inner : inner + 1, columns], spread)
                right_weight = jnp.broadcast_to(codes[inner : inner + 1, columns], spread)
                first = max(0, (tile * LANES - 1) // 2 - 2) // LANES
                last = min(width - 1, ((tile + 1) * LANES - 2) // 2 + 3) // LANES

                def value(field, index):
                    found = None
                    for piece in range(first, min(last, tiles - 1) + 1):
                        got = jnp.take_along_axis(
                            field[:, piece * LANES : (piece + 1) * LANES],
                            index & (LANES - 1),
                            axis=1,
                        )
                        if found is None:
                            found = got
                        else:
                            found = jnp.where(index >= piece * LANES, got, found)
                    return found

                for half in range(2):
                    out[block, :, half, columns] = (1.0 - right_weight) * value(
                        pair[half], left
                    ) + right_weight * value(pair[half], left + 1)
        return carry

    lax.fori_loop(0, blocks // GROUP, one_group, 0)


def per_device(
    members,
    control,
    hybrid_weight,
    member_weights,
    source_device,
    source_row,
    column_source,
    column_code,
):
    count, chans, rows, width = members.shape
    spaces, slots = lax.axis_size("space"), lax.axis_size("member")
    own_chans = chans // slots
    some = own_chans // PARTS
    chunks = PARTS * slots
    capacity = max(2, 2 * rows // spaces)
    f32 = jnp.float32
    source = source_device[:, 0]

    vmem = pl.BlockSpec(memory_space=pltpu.VMEM)
    smem = pl.BlockSpec(memory_space=pltpu.SMEM)
    anywhere = pl.BlockSpec(memory_space=pl.ANY)
    dma = pltpu.SemaphoreType.DMA
    halo = pltpu.VMEM((chans, REACH * count, width), f32)
    line = pltpu.VMEM((chans, REACH, width), f32)
    ext_rows = rows + 2 * REACH
    field = pltpu.VMEM((rows + 2 * (REACH + 2), count, width), f32)
    still = pltpu.VMEM((rows + 2 * (SWEEPS + 1), own_chans, width), f32)
    arrived = pl.pallas_call(
        functools.partial(apply_kernel, spaces, slots, capacity),
        out_shape=jax.ShapeDtypeStruct((PARTS, spaces, capacity, 2, some, width), f32),
        in_specs=[anywhere] * 2 + [smem] * 4,
        out_specs=anywhere,
        scratch_shapes=[
            pltpu.VMEM((rows * count, rows * count), jnp.bfloat16),
            pltpu.VMEM((chunks, count, some, rows, width), jnp.bfloat16),
            pltpu.VMEM((chans, rows, width), f32),
            pltpu.VMEM((count, width), f32),
            pltpu.VMEM((own_chans, width), f32),
            pltpu.VMEM((spaces, capacity, LANES), jnp.int32),
            pltpu.VMEM((2, chans, REACH, width), f32),
            halo,
            halo,
            halo,
            halo,
            line,
            line,
            pltpu.VMEM((ext_rows * count, width), f32),
            field,
            field,
            still,
            still,
            pltpu.VMEM((PARTS, slots, ext_rows, some, width), f32),
            pltpu.VMEM((PARTS, slots - 1, ext_rows, some, width), f32),
            pltpu.VMEM((PARTS, rows + 2 * SWEEPS, some, width), f32),
            pltpu.VMEM((PARTS, SWEEPS, some, width), f32),
            pltpu.VMEM((PARTS, SWEEPS + 1, some, width), f32),
            pltpu.VMEM((PARTS, rows + 1, some, width), f32),
            pltpu.VMEM((spaces - 1, capacity, LANES), jnp.int32),
            pltpu.VMEM((PARTS, spaces, capacity, 2, some, width), f32),
            dma((chunks,)),
            dma,
            dma((chans,)),
            dma((chans,)),
            dma((chans,)),
            dma((chans,)),
            dma((2,)),
            dma((2,)),
            dma((spaces - 1,)),
            dma((spaces - 1,)),
            dma((PARTS, slots - 1)),
            dma((PARTS, slots - 1)),
            dma((PARTS, 2)),
            dma((PARTS, 2)),
            dma((PARTS, spaces - 1)),
            dma((PARTS, spaces - 1)),
            dma((PARTS,)),
        ],
        compiler_params=pltpu.CompilerParams(
            collective_id=0, has_side_effects=True, vmem_limit_bytes=48 * 2**20
        ),
        name="covariance_apply",
    )(members, control, hybrid_weight, member_weights, source, source_row)

    arrived = arrived.reshape(PARTS, spaces * capacity, 2, some, width)
    return pl.pallas_call(
        functools.partial(regrid_kernel, capacity),
        out_shape=jax.ShapeDtypeStruct((rows, own_chans, 2, column_source.shape[1]), f32),
        in_specs=[smem] + [vmem] * 3,
        out_specs=vmem,
        scratch_shapes=[pltpu.SMEM((rows,), jnp.int32)],
        compiler_params=pltpu.CompilerParams(vmem_limit_bytes=32 * 2**20),
        name="regrid",
    )(source, column_source, column_code, arrived)


def solution(mesh):
    placed = (
        P("member", None, "space", None),
        P(None, "space", None),
        P(),
        P(),
        P("space", None),
        P("space"),
        P("space", None),
        P("space", None),
    )
    return jax.shard_map(
        per_device,
        mesh=mesh,
        in_specs=placed,
        out_specs=P("space", "member", None, None),
        check_vma=False,
    )
```

```python
import functools

import jax
import jax.numpy as jnp
from jax import lax
from jax.experimental import pallas as pl
from jax.experimental.pallas import tpu as pltpu
from jax.sharding import PartitionSpec as P

SWEEPS = 4
DIFFUSE = 0.2
SCALE = DIFFUSE**SWEEPS
REACH = SWEEPS // 2
LANES = 128
GROUP = 8
PARTS = 2
AHEAD = 2
MESH = pl.DeviceIdType.MESH


def beside(x):
    tiles = x.shape[1] // LANES
    lane = lax.broadcasted_iota(jnp.int32, (x.shape[0], LANES), 1)
    pieces = [x[:, tile * LANES : (tile + 1) * LANES] for tile in range(tiles)]
    ahead = [pltpu.roll(piece, 1, 1) for piece in pieces]
    behind = [pltpu.roll(piece, LANES - 1, 1) for piece in pieces]
    found = []
    for tile in range(tiles):
        left = jnp.where(lane == 0, ahead[tile - 1] if tile else 0.0, ahead[tile])
        after = behind[tile + 1] if tile + 1 < tiles else 0.0
        found.append(left + jnp.where(lane == LANES - 1, after, behind[tile]))
    return jnp.concatenate(found, axis=1)


def ranked(source_device, capacity):
    blocks = source_device.shape[0]
    devices = [source_device[block] for block in range(blocks)]
    found = []
    for block in range(blocks):
        rank = jnp.int32(0)
        for earlier in range(block):
            rank = rank + (devices[earlier] == devices[block]).astype(jnp.int32)
        found.append(devices[block] * capacity + rank)
    return found


def apply_kernel(
    spaces,
    slots,
    capacity,
    members,
    control_hbm,
    hybrid_hbm,
    weights_hbm,
    device_hbm,
    row_hbm,
    arrived,
    perm,
    states,
    control,
    hybrid_weight,
    member_weights,
    source_device,
    source_row,
    weight,
    blend,
    request,
    edges,
    turned,
    recv_low,
    recv_high,
    ctrl_low,
    ctrl_high,
    buf_a,
    buf_b,
    stat_a,
    stat_b,
    acc,
    red,
    ext,
    from_low,
    from_high,
    fin,
    asked,
    outgoing,
    load_sem,
    ctrl_sem,
    small_sem,
    up_send,
    up_recv,
    down_send,
    down_recv,
    edge_send,
    edge_recv,
    ask_send,
    ask_recv,
    red_send,
    red_recv,
    fix_send,
    fix_recv,
    out_send,
    out_recv,
    own_sem,
):
    me = lax.axis_index("space")
    slot = lax.axis_index("member")
    count, chans, rows, width = members.shape
    own_chans = chans // slots
    parts, some = acc.shape[0], acc.shape[3]
    chunks = parts * slots
    has_low = me > 0
    has_high = me < spaces - 1
    low_mask = jnp.where(has_low, 1.0, 0.0).astype(jnp.float32)
    high_mask = jnp.where(has_high, 1.0, 0.0).astype(jnp.float32)
    low, high = {"space": me - 1}, {"space": me + 1}

    def first_chan(chunk):
        owner = lax.rem(slot + 1 + chunk % slots, slots)
        return owner * own_chans + (chunk // slots) * some

    def load(chunk):
        return pltpu.make_async_copy(
            members.at[:, pl.ds(first_chan(chunk), some)], states.at[chunk], load_sem.at[chunk]
        )

    def load_control():
        return pltpu.make_async_copy(control_hbm, control, ctrl_sem)

    def load_small():
        pairs = (
            (hybrid_hbm, hybrid_weight),
            (weights_hbm, member_weights),
            (device_hbm, source_device),
            (row_hbm, source_row),
        )
        return [
            pltpu.make_async_copy(src, dst, small_sem.at[index])
            for index, (src, dst) in enumerate(pairs)
        ]

    load_control().start()
    for copy in load_small():
        copy.start()
    for chunk in range(chunks):
        load(chunk).start()

    barrier = pltpu.get_barrier_semaphore()
    for step in range(1, spaces):
        pl.semaphore_signal(
            barrier, inc=1, device_id={"space": lax.rem(me + step, spaces)}, device_id_type=MESH
        )
    for step in range(1, slots):
        pl.semaphore_signal(
            barrier, inc=1, device_id={"member": lax.rem(slot + step, slots)}, device_id_type=MESH
        )

    place = lax.broadcasted_iota(jnp.int32, perm.shape, 0)
    source = lax.broadcasted_iota(jnp.int32, perm.shape, 1)
    wanted = lax.rem(place, count) * rows + place // count
    perm[...] = jnp.where(source == wanted, 1.0, 0.0).astype(jnp.bfloat16)

    load_control().wait()
    edges[0] = control[:, :REACH, :]
    edges[1] = control[:, rows - REACH :, :]
    pl.semaphore_wait(barrier, spaces + slots - 2)

    def remote(src, dst, send, recv, device):
        return pltpu.make_async_remote_copy(
            src_ref=src,
            dst_ref=dst,
            send_sem=send,
            recv_sem=recv,
            device_id=device,
            device_id_type=MESH,
        )

    def edge_up():
        return remote(edges.at[0], ctrl_high, edge_send.at[0], edge_recv.at[0], low)

    def edge_down():
        return remote(edges.at[1], ctrl_low, edge_send.at[1], edge_recv.at[1], high)

    span = REACH * count

    def halo_up(turn):
        return remote(
            turned.at[turn, pl.ds(0, span)], recv_high.at[turn], up_send.at[turn], up_recv.at[turn], low
        )

    def halo_down(turn):
        return remote(
            turned.at[turn, pl.ds((rows - REACH) * count, span)],
            recv_low.at[turn],
            down_send.at[turn],
            down_recv.at[turn],
            high,
        )

    def ask(step):
        target = lax.rem(me + step, spaces)
        return remote(
            request.at[target],
            asked.at[step - 1],
            ask_send.at[step - 1],
            ask_recv.at[step - 1],
            {"space": target},
        )

    @pl.when(has_low)
    def _():
        edge_up().start()

    @pl.when(has_high)
    def _():
        edge_down().start()

    def turn_over(chunk, index):
        flat = states[chunk, :, index].reshape(count * rows, width)
        turned[chunk * some + index] = jnp.dot(
            perm[...], flat, preferred_element_type=jnp.float32
        )

    def send_edges(chunk, index):
        turn = chunk * some + index

        @pl.when(has_low)
        def _():
            halo_up(turn).start()

        @pl.when(has_high)
        def _():
            halo_down(turn).start()

    for chunk in range(AHEAD):
        load(chunk).wait()

        def ahead(index, carry, chunk=chunk):
            turn_over(chunk, index)
            send_edges(chunk, index)
            return carry

        lax.fori_loop(0, some, ahead, 0)
    for copy in load_small():
        copy.wait()

    shape = request.shape
    number = lax.broadcasted_iota(jnp.int32, shape, 0) * capacity
    number = number + lax.broadcasted_iota(jnp.int32, shape, 1)
    needs = jnp.zeros(shape, jnp.int32)
    for block, at in enumerate(ranked(source_device, capacity)):
        needs = jnp.where(number == at, source_row[block], needs)
    request[...] = needs
    for step in range(1, spaces):
        ask(step).start()

    total = lax.fori_loop(
        0,
        member_weights.shape[0],
        lambda index, so_far: so_far + member_weights[index],
        jnp.int32(0),
    )
    which = lax.broadcasted_iota(jnp.int32, weight.shape, 0)
    value = jnp.zeros(weight.shape, jnp.float32)
    for index in range(count):
        code = member_weights[slot * count + index].astype(jnp.float32)
        value = jnp.where(which == index, code, value)
    weight[...] = value / jnp.full(weight.shape, total.astype(jnp.float32)) * SCALE
    which = lax.broadcasted_iota(jnp.int32, blend.shape, 0)
    value = jnp.zeros(blend.shape, jnp.float32)
    for index in range(own_chans):
        value = jnp.where(which == index, hybrid_weight[slot * own_chans + index], value)
    blend[...] = value

    @pl.when(jnp.logical_not(has_low))
    def _():
        recv_low[...] = jnp.zeros_like(recv_low)
        ctrl_low[...] = jnp.zeros_like(ctrl_low)
        from_low[...] = jnp.zeros_like(from_low)

    @pl.when(jnp.logical_not(has_high))
    def _():
        recv_high[...] = jnp.zeros_like(recv_high)
        ctrl_high[...] = jnp.zeros_like(ctrl_high)
        from_high[...] = jnp.zeros_like(from_high)

    def swept(ref, at):
        middle = ref[at]
        return ref[at - 1] + ref[at + 1] + (middle + beside(middle))

    def masked(value, row):
        if row < 0:
            return value * low_mask
        if row >= rows:
            return value * high_mask
        return value

    stat_a[...] = jnp.zeros_like(stat_a)
    stat_b[...] = jnp.zeros_like(stat_b)
    margin = SWEEPS + 1
    for index in range(own_chans):
        field = control[slot * own_chans + index]
        for row in range(rows):
            stat_a[margin + row, pl.ds(index, 1), :] = field[row : row + 1]
    here, there = stat_a, stat_b
    for sweep in range(1, SWEEPS + 1):
        for row in range(-sweep, rows + sweep):
            there[margin + row] = masked(swept(here, margin + row), row)
        here, there = there, here
    static = here

    buf_a[...] = jnp.zeros_like(buf_a)
    buf_b[...] = jnp.zeros_like(buf_b)
    base = REACH + 2

    @pl.when(has_low)
    def _():
        edge_down().wait_recv()

    @pl.when(has_high)
    def _():
        edge_up().wait_recv()

    def give(part, group):
        return remote(
            acc.at[part, group],
            red.at[part, group],
            red_send.at[part, group],
            red_recv.at[part, group],
            {"member": lax.rem(slot + 1 + group, slots)},
        )

    def fix_up(part):
        return remote(
            ext.at[part, pl.ds(0, SWEEPS + 1)],
            from_high.at[part],
            fix_send.at[part, 0],
            fix_recv.at[part, 0],
            low,
        )

    def fix_down(part):
        return remote(
            ext.at[part, pl.ds(rows + SWEEPS, SWEEPS)],
            from_low.at[part],
            fix_send.at[part, 1],
            fix_recv.at[part, 1],
            high,
        )

    def answer(part, step):
        target = lax.rem(me + spaces - step, spaces)
        return remote(
            outgoing.at[part, step],
            arrived.at[part, me],
            out_send.at[part, step - 1],
            out_recv.at[part, step - 1],
            {"space": target},
        )

    def keep(part):
        return pltpu.make_async_copy(
            outgoing.at[part, 0], arrived.at[part, me], own_sem.at[part]
        )

    def combine(part):
        for group in range(slots - 1):
            give(part, group).wait_recv()
        mine = slice(part * some, (part + 1) * some)
        share = blend[mine, :]
        for row in range(-SWEEPS, rows + SWEEPS):
            value = (share * SCALE) * static[margin + row, mine, :]
            if -REACH <= row < rows + REACH:
                total = acc[part, slots - 1, row + REACH]
                for group in range(slots - 1):
                    total = total + red[part, group, row + REACH]
                value = value + (1.0 - share) * total
            ext[part, row + SWEEPS] = value

        @pl.when(has_low)
        def _():
            fix_up(part).start()

        @pl.when(has_high)
        def _():
            fix_down(part).start()

    def fill(part, step, wants):
        for place in range(capacity):
            line = jnp.concatenate([wants[place]] * (width // LANES), axis=1)
            line = jnp.broadcast_to(line, (some, width))
            lower, upper = fin[part, 0], fin[part, 1]
            for row in range(1, rows):
                hit = line == row
                lower = jnp.where(hit, fin[part, row], lower)
                upper = jnp.where(hit, fin[part, row + 1], upper)
            outgoing[part, step, place, 0] = lower
            outgoing[part, step, place, 1] = upper

    def serve(part):
        @pl.when(has_low)
        def _():
            fix_down(part).wait_recv()

        @pl.when(has_high)
        def _():
            fix_up(part).wait_recv()

        for row in range(rows + 1):
            value = ext[part, row + SWEEPS]
            if row < SWEEPS:
                value = value + from_low[part, row]
            if row >= rows - SWEEPS:
                value = value + from_high[part, row - rows + SWEEPS]
            fin[part, row] = value
        if part == 0:
            for step in range(1, spaces):
                ask(step).wait_recv()
        for step in sorted(range(1, spaces), key=lambda step: -min(step, spaces - step)):
            fill(part, step, [asked[step - 1, pl.ds(p, 1), :] for p in range(capacity)])
            answer(part, step).start()
        fill(part, 0, [request[me, pl.ds(p, 1), :] for p in range(capacity)])
        keep(part).start()

    for chunk in range(chunks):
        part, group = chunk // slots, chunk % slots
        if chunk + AHEAD < chunks:
            load(chunk + AHEAD).wait()

        def one_channel(index, carry, chunk=chunk, part=part, group=group):
            turn = chunk * some + index
            chan = first_chan(chunk) + index

            @pl.when(has_low)
            def _():
                halo_down(turn).wait_recv()

            @pl.when(has_high)
            def _():
                halo_up(turn).wait_recv()

            def state(row):
                if row < 0:
                    return recv_low[turn, pl.ds((row + REACH) * count, count), :]
                if row >= rows:
                    return recv_high[turn, pl.ds((row - rows) * count, count), :]
                return turned[turn, pl.ds(row * count, count), :]

            for row in range(-REACH, rows + REACH):
                if row < 0:
                    line = ctrl_low[chan, pl.ds(row + REACH, 1), :]
                elif row >= rows:
                    line = ctrl_high[chan, pl.ds(row - rows, 1), :]
                else:
                    line = control[chan, pl.ds(row, 1), :]
                buf_a[base + row] = state(row) * line

            def collect(row, value):
                total = jnp.sum(state(row) * value * weight[...], axis=0, keepdims=True)
                acc[part, group, row + REACH, pl.ds(index, 1), :] = total

            for outer, inner, away in ((-1, 2, 1), (rows, rows - 3, -1)):
                near = buf_a[base + inner]
                far = buf_a[base + inner + away]
                collect(outer, SWEEPS * (near + beside(near)) + far)
                collect(outer - away, near)

            for row in range(-3, rows + 3):
                buf_b[base + row] = masked(swept(buf_a, base + row), row)
            for row in range(-2, rows + 2):
                buf_a[base + row] = masked(swept(buf_b, base + row), row)
            for row in range(-1, rows + 1):
                buf_b[base + row] = masked(swept(buf_a, base + row), row)
            for row in range(rows):
                collect(row, swept(buf_b, base + row))
            if chunk + AHEAD < chunks:
                turn_over(chunk + AHEAD, index)
                send_edges(chunk + AHEAD, index)
            return carry

        lax.fori_loop(0, some, one_channel, 0)
        if group < slots - 1:
            give(part, group).start()
        else:
            combine(part)
        if group == 0 and part > 0:
            serve(part - 1)

    serve(parts - 1)

    for part in range(parts):
        for step in range(1, spaces):
            answer(part, step).wait_recv()
        keep(part).wait()
        for step in range(1, spaces):
            answer(part, step).wait_send()
        for group in range(slots - 1):
            give(part, group).wait_send()

        @pl.when(has_low)
        def _():
            fix_up(part).wait_send()

        @pl.when(has_high)
        def _():
            fix_down(part).wait_send()

    for step in range(1, spaces):
        ask(step).wait_send()

    @pl.when(has_low)
    def _():
        edge_up().wait_send()

    @pl.when(has_high)
    def _():
        edge_down().wait_send()

    def drain(turn, carry):
        @pl.when(has_low)
        def _():
            halo_up(turn).wait_send()

        @pl.when(has_high)
        def _():
            halo_down(turn).wait_send()

        return carry

    lax.fori_loop(0, chans, drain, 0)


def regrid_kernel(capacity, source_device, column_source, column_code, arrived, out, slot_index):
    blocks, fine = column_source.shape
    parts, some, width = arrived.shape[0], arrived.shape[3], arrived.shape[4]
    chans = parts * some
    tiles = width // LANES
    for block, at in enumerate(ranked(source_device, capacity)):
        slot_index[block] = at

    def one_group(group, carry):
        lines = pl.ds(pl.multiple_of(group * GROUP, GROUP), GROUP)
        sources = column_source[lines, :]
        codes = column_code[lines, :].astype(jnp.float32) / 16.0
        for inner in range(GROUP):
            block = group * GROUP + inner
            at = slot_index[block]
            lower = jnp.concatenate([arrived[part, at, 0] for part in range(parts)], axis=0)
            upper = jnp.concatenate([arrived[part, at, 1] for part in range(parts)], axis=0)
            pair = (0.75 * lower + 0.25 * upper, 0.25 * lower + 0.75 * upper)
            for tile in range(fine // LANES):
                columns = slice(tile * LANES, (tile + 1) * LANES)
                spread = (chans, LANES)
                left = jnp.broadcast_to(sources[inner : inner + 1, columns], spread)
                right_weight = jnp.broadcast_to(codes[inner : inner + 1, columns], spread)
                first = max(0, (tile * LANES - 1) // 2 - 2) // LANES
                last = min(width - 1, ((tile + 1) * LANES - 2) // 2 + 3) // LANES

                def value(field, index):
                    found = None
                    for piece in range(first, min(last, tiles - 1) + 1):
                        got = jnp.take_along_axis(
                            field[:, piece * LANES : (piece + 1) * LANES],
                            index & (LANES - 1),
                            axis=1,
                        )
                        if found is None:
                            found = got
                        else:
                            found = jnp.where(index >= piece * LANES, got, found)
                    return found

                for half in range(2):
                    out[block, :, half, columns] = (1.0 - right_weight) * value(
                        pair[half], left
                    ) + right_weight * value(pair[half], left + 1)
        return carry

    lax.fori_loop(0, blocks // GROUP, one_group, 0)


def per_device(
    members,
    control,
    hybrid_weight,
    member_weights,
    source_device,
    source_row,
    column_source,
    column_code,
):
    count, chans, rows, width = members.shape
    spaces, slots = lax.axis_size("space"), lax.axis_size("member")
    own_chans = chans // slots
    some = own_chans // PARTS
    chunks = PARTS * slots
    capacity = max(2, 2 * rows // spaces)
    f32 = jnp.float32
    source = source_device[:, 0]

    vmem = pl.BlockSpec(memory_space=pltpu.VMEM)
    smem = pl.BlockSpec(memory_space=pltpu.SMEM)
    anywhere = pl.BlockSpec(memory_space=pl.ANY)
    dma = pltpu.SemaphoreType.DMA
    halo = pltpu.VMEM((chans, REACH * count, width), f32)
    line = pltpu.VMEM((chans, REACH, width), f32)
    ext_rows = rows + 2 * REACH
    field = pltpu.VMEM((rows + 2 * (REACH + 2), count, width), f32)
    still = pltpu.VMEM((rows + 2 * (SWEEPS + 1), own_chans, width), f32)
    arrived = pl.pallas_call(
        functools.partial(apply_kernel, spaces, slots, capacity),
        out_shape=jax.ShapeDtypeStruct((PARTS, spaces, capacity, 2, some, width), f32),
        in_specs=[pl.BlockSpec(memory_space=pltpu.HBM)] * 6,
        out_specs=anywhere,
        scratch_shapes=[
            pltpu.VMEM((rows * count, rows * count), jnp.bfloat16),
            pltpu.VMEM((chunks, count, some, rows, width), jnp.bfloat16),
            pltpu.VMEM((chans, rows, width), f32),
            pltpu.SMEM(hybrid_weight.shape, f32),
            pltpu.SMEM(member_weights.shape, jnp.int32),
            pltpu.SMEM(source.shape, jnp.int32),
            pltpu.SMEM(source.shape, jnp.int32),
            pltpu.VMEM((count, width), f32),
            pltpu.VMEM((own_chans, width), f32),
            pltpu.VMEM((spaces, capacity, LANES), jnp.int32),
            pltpu.VMEM((2, chans, REACH, width), f32),
            pltpu.VMEM((chans, rows * count, width), f32),
            halo,
            halo,
            line,
            line,
            field,
            field,
            still,
            still,
            pltpu.VMEM((PARTS, slots, ext_rows, some, width), f32),
            pltpu.VMEM((PARTS, slots - 1, ext_rows, some, width), f32),
            pltpu.VMEM((PARTS, rows + 2 * SWEEPS, some, width), f32),
            pltpu.VMEM((PARTS, SWEEPS, some, width), f32),
            pltpu.VMEM((PARTS, SWEEPS + 1, some, width), f32),
            pltpu.VMEM((PARTS, rows + 1, some, width), f32),
            pltpu.VMEM((spaces - 1, capacity, LANES), jnp.int32),
            pltpu.VMEM((PARTS, spaces, capacity, 2, some, width), f32),
            dma((chunks,)),
            dma,
            dma((4,)),
            dma((chans,)),
            dma((chans,)),
            dma((chans,)),
            dma((chans,)),
            dma((2,)),
            dma((2,)),
            dma((spaces - 1,)),
            dma((spaces - 1,)),
            dma((PARTS, slots - 1)),
            dma((PARTS, slots - 1)),
            dma((PARTS, 2)),
            dma((PARTS, 2)),
            dma((PARTS, spaces - 1)),
            dma((PARTS, spaces - 1)),
            dma((PARTS,)),
        ],
        compiler_params=pltpu.CompilerParams(
            collective_id=0, has_side_effects=True, vmem_limit_bytes=64 * 2**20
        ),
        name="covariance_apply",
    )(members, control, hybrid_weight, member_weights, source, source_row)

    arrived = arrived.reshape(PARTS, spaces * capacity, 2, some, width)
    return pl.pallas_call(
        functools.partial(regrid_kernel, capacity),
        out_shape=jax.ShapeDtypeStruct((rows, own_chans, 2, column_source.shape[1]), f32),
        in_specs=[smem] + [vmem] * 3,
        out_specs=vmem,
        scratch_shapes=[pltpu.SMEM((rows,), jnp.int32)],
        compiler_params=pltpu.CompilerParams(vmem_limit_bytes=32 * 2**20),
        name="regrid",
    )(source, column_source, column_code, arrived)


def solution(mesh):
    placed = (
        P("member", None, "space", None),
        P(None, "space", None),
        P(),
        P(),
        P("space", None),
        P("space"),
        P("space", None),
        P("space", None),
    )
    return jax.shard_map(
        per_device,
        mesh=mesh,
        in_specs=placed,
        out_specs=P("space", "member", None, None),
        check_vma=False,
    )
```
